512 devices in a mesh: dp: 16 (over y, core), expert: 8 (over z), mp: 4 (over x).
Axes of the slice: x: 4, y: 8, z: 8, core: 2. Of those that a mesh axis runs over, the one named last changes fastest.
Arguments:
- tokens: bfloat16 [2048, 4096], P('dp', 'mp'), may hold values from -6 to 6
- slot_ids: int32 [2048, 2], P('dp'), may hold values from 0 to 7, all different within a row; in each aligned block of 128 rows (0 to 127, 128 to 255, ...) at most 40 rows name the same one
- gate_values: float32 [2048, 2], P('dp'), may hold values from 0.2 to 1
- slot_expert: int32 [8], replicated, may hold values from 0 to 3, as said below
- w_gate: bfloat16 [4, 7168, 4096], P(None, ('dp', 'expert'), 'mp'), may hold values from -0.09375 to 0.09375
- w_up: bfloat16 [4, 7168, 4096], P(None, ('dp', 'expert'), 'mp'), may hold values from -0.09375 to 0.09375
- w_down: bfloat16 [4, 7168, 4096], P(None, ('dp', 'expert'), 'mp'), may hold values from -0.0625 to 0.0625
- cotangent: bfloat16 [2048, 4096], P('dp', 'mp'), may hold values from -6 to 6
Outputs:
- mixed: bfloat16 [2048, 4096], P('dp', 'mp')
- grad_tokens: bfloat16 [2048, 4096], P('dp', 'mp')
- grad_gate: bfloat16 [4, 7168, 4096], P(None, ('dp', 'expert'), 'mp')
- grad_up: bfloat16 [4, 7168, 4096], P(None, ('dp', 'expert'), 'mp')
- grad_down: bfloat16 [4, 7168, 4096], P(None, ('dp', 'expert'), 'mp')
The draws below stay inside these ranges and needn't reach their ends.
Inputs may be any that keep to these rules, and one draw needn't show every extreme that they name: `slot_ids`: the two slots of a token differ. Among the tokens of one index of dp no slot is named more than 40 times, a bound that some block reaches in some of them. `slot_expert`: every one of the 4 experts is held by one slot or more.
All inputs are finite; a program needn't handle non-finite values.
Results may differ from the reference program's by a relative error of at most 0.024.
Values may be sent and summed in bfloat16 or wider, within the bound.
No kernel may reach another device: no remote copies, remote signals or barrier semaphores. Data moves between devices by JAX's collectives and lax.ppermute only.
A program may use at most 64 MiB of HBM per device.

```python
import math
import jax
import jax.numpy as jnp
import numpy as np
from jax import lax

D = 4096
F = 7168
TOP = 2
TOK_DEV = 128
TOKENS = 2048
EXPERTS = 4
SLOTS = 8
CAP = 40
N_DP = 16
N_MP = 4


def draw_slot_expert(key, part):
    key = jax.random.fold_in(key, 7)
    first_key, second_key = jax.random.split(key)
    extra = jax.random.randint(first_key, (SLOTS - EXPERTS,), 0, EXPERTS, dtype=jnp.int32)
    values = jnp.concatenate([jnp.arange(EXPERTS, dtype=jnp.int32), extra])
    shuffle = jax.random.permutation(second_key, SLOTS)
    return values[shuffle].astype(jnp.int32)


def block_scale(rng, extent, shards, smallest, high):
    level = 1.0
    for dim, shards_of in shards:
        heights = jax.random.uniform(jax.random.fold_in(jax.random.fold_in(rng, 6), dim), (shards_of,), jnp.float32, smallest / len(shards), high / len(shards))
        level = level * jnp.repeat(jnp.exp(heights), extent[dim] // shards_of).reshape((-1,) + (1,) * (len(extent) - 1 - dim))
    return level


def routed_block(own_key, own, number, rows, number_of, top, reach, skew):
    ranking = jax.random.permutation(own_key, number_of)
    packed, ordinary = portions_of(number_of, rows * top, reach, skew, True), portions_of(number_of, rows * top, reach, skew, False)
    places = jnp.arange(number_of)

    def named(sizes, offset_by):
        used = int((sizes > 0).sum())
        fixed = max(1, used // 4)
        shifted = fixed + (places - fixed + offset_by * (used - fixed)) % max(1, number_of - fixed)
        return jnp.zeros((number_of,), jnp.int32).at[ranking[jnp.where(places < fixed, places, shifted)]].set(jnp.asarray(sizes, jnp.int32))

    sizes = jnp.where(number % 4 == 0, named(packed, number // 4), named(ordinary, number - number // 4 - 1))
    mixed = jax.random.permutation(jax.random.fold_in(own, 3), number_of)
    source_of, taker = mixed[0:number_of // 2 * 2:2], mixed[1:number_of // 2 * 2:2]
    margin = jnp.minimum(sizes[source_of] - 1, reach - sizes[taker]) // 2
    margin = jnp.where((source_of == ranking[0]) | (taker == ranking[0]) | (sizes[taker] == 0), 0, jnp.maximum(margin, 0))
    shifted = jax.random.randint(jax.random.fold_in(own, 4), (number_of // 2,), 0, 1 << 20) % (margin + 1)
    sizes = sizes.at[source_of].add(-shifted).at[taker].add(shifted)
    members = jnp.searchsorted(jnp.cumsum(sizes), jnp.arange(rows * top), side="right").astype(jnp.int32)
    grid = members.reshape(top, rows).T
    grid = grid[jax.random.permutation(jax.random.fold_in(own, 1), rows)]
    offset_by = jax.random.randint(jax.random.fold_in(own, 2), (rows, 1), 0, top)
    return jnp.take_along_axis(grid, (jnp.arange(top)[None, :] + offset_by) % top, axis=1)


def portions_of(number_of, total, most, lean, full):
    weights = [(1 << 20) // math.isqrt(rank ** lean) + 1 for rank in range(1, number_of + 1)]
    largest = most if full else min(most, max(-(-total // number_of), total * weights[0] // sum(weights)))
    least = 1 if total - largest >= number_of - 1 else 0
    counts, surplus = [largest] + [least] * (number_of - 1), total - largest - least * (number_of - 1)
    while surplus > 0:
        candidates = [i for i in range(1, number_of) if counts[i] < largest] or [i for i in range(1, number_of) if counts[i] < most]
        mass, remaining = sum([weights[i] for i in candidates]), surplus
        for i in candidates:
            addition = min(most - counts[i], max(1, remaining * weights[i] // mass), surplus)
            counts[i] = counts[i] + addition
            surplus = surplus - addition
    return np.array(counts)


def centred(key, extent, scale, limit, shards=(), kind=jnp.bfloat16):
    array = jax.random.normal(key, extent, jnp.float32) * scale
    if len(shards) > 0:
        array = block_scale(key, extent, shards, -0.22, 0.18) * array
    return jnp.clip(array, min=-limit, max=limit).astype(kind)


def setup_inputs(seed: int = 0) -> dict:
    key_list = jax.random.split(jax.random.key(seed), 9)
    tokens = centred(key_list[0], (TOKENS, D), 1.0, 6.0, ((0, 16), (1, 4)))
    slot_ids_keys = jax.random.split(jax.random.fold_in(key_list[1], 1), TOKENS // TOK_DEV)
    slot_ids_turns = jax.random.permutation(jax.random.fold_in(key_list[1], 3), TOKENS // TOK_DEV)
    slot_ids = jax.vmap(lambda own, number: routed_block(jax.random.fold_in(key_list[1], 2), own, number, TOK_DEV, SLOTS, TOP, CAP, 2))(slot_ids_keys, slot_ids_turns).reshape((TOKENS, TOP))
    gate_values = jnp.clip(0.2 + 0.8 * jax.random.uniform(key_list[2], (TOKENS, TOP), jnp.float32) ** block_scale(key_list[2], (TOKENS, TOP), ((0, 16),), -0.2, 0.2), 0.2, 1.0)
    slot_expert = draw_slot_expert(jax.random.fold_in(key_list[8], 71), 0)
    w_gate = centred(key_list[4], (EXPERTS, F, D), D ** -0.5, 0.09375, ((1, 128), (2, 4)))
    w_up = centred(key_list[5], (EXPERTS, F, D), D ** -0.5, 0.09375, ((1, 128), (2, 4)))
    w_down = centred(key_list[6], (EXPERTS, F, D), F ** -0.5, 0.0625, ((1, 128), (2, 4)))
    cotangent = centred(key_list[7], (TOKENS, D), 1.0, 6.0, ((0, 16), (1, 4)))
    return {"tokens": tokens, "slot_ids": slot_ids, "gate_values": gate_values, "slot_expert": slot_expert, "w_gate": w_gate, "w_up": w_up, "w_down": w_down, "cotangent": cotangent}


def split_sum(rows, matrix):
    blocks = jnp.einsum("rmd,mdf->rmf", rows.reshape(rows.shape[0], N_MP, -1), matrix.reshape(N_MP, -1, matrix.shape[1]))
    rounded = lax.optimization_barrier(blocks.astype(jnp.bfloat16))
    return jnp.sum(rounded.astype(jnp.float32), axis=1)


def rounded_f32(values):
    return lax.optimization_barrier(values.astype(jnp.bfloat16)).astype(jnp.float32)


def reference(tokens, slot_ids, gate_values, slot_expert, w_gate, w_up, w_down, cotangent):
    total_rows = N_DP * CAP
    flattened = slot_ids.reshape(-1)
    weights_flat = gate_values.reshape(-1)
    width = tokens.shape[1]
    hidden_units = w_gate.shape[1]
    experts = w_gate.shape[0]

    def one_slot(carry, slot):
        mixed_sum, token_grad, grad_gate, grad_up, grad_down = carry
        chosen = flattened == slot
        count = jnp.sum(chosen.astype(jnp.int32))
        entries = jnp.nonzero(chosen, size=total_rows, fill_value=0)[0]
        valid = jnp.arange(total_rows) < count
        token_index = (entries // 2).astype(jnp.int32)
        scales = jnp.where(valid, weights_flat[entries], jnp.float32(0.0))
        rows_bf = jnp.where(valid[:, None], tokens[token_index], jnp.zeros((), jnp.bfloat16))
        rows = rows_bf.astype(jnp.float32)
        expert = slot_expert[slot]
        gate_matrix = w_gate[expert]
        up_matrix = w_up[expert]
        down_matrix = w_down[expert]
        gate = split_sum(rows, gate_matrix.astype(jnp.float32).T)
        up_val = split_sum(rows, up_matrix.astype(jnp.float32).T)
        sigm = jax.nn.sigmoid(gate)
        active = gate * sigm
        hidden = (active * up_val).astype(jnp.bfloat16)
        output = jnp.dot(hidden, down_matrix, preferred_element_type=jnp.float32)
        mixed_sum = mixed_sum.at[token_index].add(scales[:, None] * output)
        upstream = (scales[:, None] * cotangent[token_index].astype(jnp.float32)).astype(jnp.bfloat16)
        grad_hidden = split_sum(upstream.astype(jnp.float32), down_matrix.astype(jnp.float32).T)
        grad_gatev = (grad_hidden * up_val * sigm * (1.0 + gate * (1.0 - sigm))).astype(jnp.bfloat16)
        grad_upv = (grad_hidden * active).astype(jnp.bfloat16)
        back = jnp.dot(grad_gatev, gate_matrix, preferred_element_type=jnp.float32)
        back = back + jnp.dot(grad_upv, up_matrix, preferred_element_type=jnp.float32)
        token_grad = token_grad.at[token_index].add(back)
        part_gate = rounded_f32(jnp.dot(grad_gatev.T, rows_bf, preferred_element_type=jnp.float32))
        part_up = rounded_f32(jnp.dot(grad_upv.T, rows_bf, preferred_element_type=jnp.float32))
        part_down = rounded_f32(jnp.dot(hidden.T, upstream, preferred_element_type=jnp.float32))
        grad_gate = grad_gate.at[expert].add(part_gate)
        grad_up = grad_up.at[expert].add(part_up)
        grad_down = grad_down.at[expert].add(part_down)
        return (mixed_sum, token_grad, grad_gate, grad_up, grad_down), None

    start = (jnp.zeros(tokens.shape, jnp.float32), jnp.zeros(tokens.shape, jnp.float32),
             jnp.zeros((experts, hidden_units, width), jnp.float32),
             jnp.zeros((experts, hidden_units, width), jnp.float32),
             jnp.zeros((experts, hidden_units, width), jnp.float32))
    final, unused = lax.scan(one_slot, start, jnp.arange(SLOTS, dtype=jnp.int32))
    mixed_sum, token_grad, grad_gate, grad_up, grad_down = final
    return (mixed_sum.astype(jnp.bfloat16), token_grad.astype(jnp.bfloat16), grad_gate.astype(jnp.bfloat16),
            grad_up.astype(jnp.bfloat16), grad_down.astype(jnp.bfloat16))
```

```python
import jax
import jax.numpy as jnp
from jax import lax
from jax.sharding import Mesh, PartitionSpec as P

F32 = jnp.float32
BF16 = jnp.bfloat16


def short(value):
    return lax.reduce_precision(value, exponent_bits=8, mantissa_bits=7)


def swap_cores(value):
    return lax.ppermute(value, "core", [(0, 1), (1, 0)])


def contract_last(left, right):
    return lax.dot_general(left, right, (((1,), (1,)), ((), ())), preferred_element_type=F32)


def contract_first(left, right):
    return lax.dot_general(left, right, (((0,), (0,)), ((), ())), preferred_element_type=F32)


def spread(value, axis):
    count = lax.axis_size(axis)
    copies = jnp.broadcast_to(value[None], (count,) + value.shape)
    copies = lax.optimization_barrier(copies)
    return lax.all_to_all(copies, axis, split_axis=0, concat_axis=0, tiled=True)


def body(tokens, slot_ids, gate_values, slot_expert, w_gate, w_up, w_down, cotangent):
    rows, width = tokens.shape
    experts, units, _ = w_gate.shape
    ny, nz, nx = lax.axis_size("y"), lax.axis_size("z"), lax.axis_size("x")
    top = slot_ids.shape[1]
    total = ny * rows
    both = 2 * units

    chosen = jnp.sum(
        jnp.where(
            slot_ids[:, :, None] == jnp.arange(slot_expert.shape[0], dtype=jnp.int32),
            slot_expert[None, None, :],
            0,
        ),
        axis=-1,
    ).astype(F32)
    part0 = short(gate_values)
    part1 = short(gate_values - part0)
    part2 = short(gate_values - part0 - part1)
    meta = jnp.stack([chosen, part0, part1, part2]).transpose(0, 2, 1).astype(BF16)
    meta = jnp.pad(meta.reshape(1, 4 * top * rows), ((0, 15), (0, width - 4 * top * rows)))
    packed = jnp.concatenate([tokens, cotangent, meta], axis=0)
    held = packed.shape[0]
    everything = lax.all_gather(packed, "y", axis=0, tiled=True).reshape(ny, held, width)

    own = jnp.stack([w_gate, w_up, w_down])
    other = swap_cores(own)
    weights = jnp.concatenate([own, other], axis=2).reshape(3, experts * both, width)

    rows_x = everything[:, :rows].reshape(total, width)
    rows_c = everything[:, rows : 2 * rows].reshape(total, width)
    facts = everything[:, 2 * rows, : 4 * top * rows].reshape(ny, 4, top, rows).astype(F32)
    facts = facts.transpose(1, 2, 0, 3).reshape(4, top, total)
    expert_of = facts[0]
    scale = facts[1] + facts[2] + facts[3]
    mask = expert_of[None] == jnp.arange(experts, dtype=F32)[:, None, None]

    def pick(weight, values):
        sums = contract_last(weight, values).astype(BF16).reshape(experts, both, total)
        return [
            sum(
                jnp.where(mask[e, k][None], sums[e], jnp.zeros((), BF16)) for e in range(experts)
            )
            for k in range(top)
        ]

    picked = jnp.stack(
        pick(weights[0], rows_x) + pick(weights[1], rows_x) + pick(weights[2], rows_c)
    )
    share = total // nx
    picked = picked.reshape(3 * top * both, nx, share).transpose(1, 0, 2)
    arrived = lax.all_to_all(picked, "x", split_axis=0, concat_axis=0, tiled=True)
    summed = jnp.sum(arrived.astype(F32), axis=0).reshape(3, top, both, share)
    gate, up, dh = summed[0], summed[1], summed[2]
    own_scale = lax.dynamic_slice_in_dim(scale, lax.axis_index("x") * share, share, axis=1)[:, None]
    dh = own_scale * dh
    sg = jax.nn.sigmoid(gate)
    active = gate * sg
    hidden = own_scale * (active * up)
    dgate = dh * up * sg * (1.0 + gate * (1.0 - sg))
    dup = dh * active
    mine = jnp.stack([hidden, dgate, dup]).astype(BF16).reshape(3 * top * both, share)
    shared = spread(mine, "x").reshape(nx, 3, top, both, share)

    def expand(which):
        values = shared[:, which].transpose(1, 2, 0, 3).reshape(top, both, total)
        wide = [
            sum(jnp.where(mask[e, k][None], values[k], jnp.zeros((), BF16)) for k in range(top))
            for e in range(experts)
        ]
        return jnp.stack(wide).reshape(experts * both, total)

    hidden_all, dgate_all, dup_all = expand(0), expand(1), expand(2)
    mixed_part = contract_first(hidden_all, weights[2]).astype(BF16)
    mixed_y = lax.psum_scatter(mixed_part, "y", scatter_dimension=0, tiled=True)
    back_part = (
        contract_first(dgate_all, weights[0]) + contract_first(dup_all, weights[1])
    ).astype(BF16)
    back = lax.all_to_all(
        back_part.reshape(ny * nz, rows // nz, width),
        ("y", "z"),
        split_axis=0,
        concat_axis=0,
        tiled=True,
    )
    back = jnp.sum(back.astype(F32), axis=0)
    mixed = lax.all_to_all(
        mixed_y.reshape(nz, rows // nz, width), "z", split_axis=0, concat_axis=0, tiled=True
    )
    mixed = jnp.sum(mixed.astype(F32), axis=0)
    ends = spread(jnp.stack([mixed, back]).astype(BF16), "z")
    mixed_out = ends[:, 0].reshape(rows, width)
    back_out = ends[:, 1].reshape(rows, width)

    def weight_gradient(left, right):
        part = jnp.dot(left, right, preferred_element_type=F32)
        return part.reshape(experts, 2, units, width)

    parts = [
        weight_gradient(dgate_all, rows_x),
        weight_gradient(dup_all, rows_x),
        weight_gradient(hidden_all, rows_c),
    ]
    sent = swap_cores(jnp.stack([part[:, 1] for part in parts]).astype(BF16))
    gradients = [
        (part[:, 0].astype(BF16).astype(F32) + sent[i].astype(F32)).astype(BF16) for i, part in enumerate(parts)
    ]
    return (mixed_out, back_out, gradients[0], gradients[1], gradients[2])


def solution(mesh):
    dp, ep, mp = mesh.shape["dp"], mesh.shape["expert"], mesh.shape["mp"]
    split = Mesh(mesh.devices.reshape(dp // 2, 2, ep, mp), ("y", "core", "z", "x"))
    rows = ("y", "core")
    stored = P(None, ("y", "core", "z"), "x")
    return jax.shard_map(
        body,
        mesh=split,
        in_specs=(
            P(rows, "x"),
            P(rows, None),
            P(rows, None),
            P(),
            stored,
            stored,
            stored,
            P(rows, "x"),
        ),
        out_specs=(P(rows, "x"), P(rows, "x"), stored, stored, stored),
        check_vma=False,
    )
```

```python
import functools
import jax
import jax.numpy as jnp
from jax import lax
from jax.experimental import pallas as pl
from jax.experimental.pallas import tpu as pltpu
from jax.sharding import Mesh, PartitionSpec as P

F32 = jnp.float32
BF16 = jnp.bfloat16
VMEM_BYTES = 48 * 1024 * 1024


def short(value):
    return lax.reduce_precision(value, exponent_bits=8, mantissa_bits=7)


def swap(value, axis):
    return lax.ppermute(value, axis, [(0, 1), (1, 0)])


def contract_last(left, right):
    return lax.dot_general(left, right, (((1,), (1,)), ((), ())), preferred_element_type=F32)


def contract_first(left, right):
    return lax.dot_general(left, right, (((0,), (0,)), ((), ())), preferred_element_type=F32)


def spread(value, axis, count):
    copies = jnp.broadcast_to(value[None], (count,) + value.shape)
    copies = lax.optimization_barrier(copies)
    return lax.all_to_all(copies, axis, split_axis=0, concat_axis=0, tiled=True)


def pick_kernel(mats, top, nx, weight_ref, rows_ref, mask_ref, out_ref):
    expert = pl.program_id(0)
    rows = rows_ref[...].reshape(-1, rows_ref.shape[2])
    share = rows.shape[0] // nx
    mask = mask_ref[0]
    for m in range(mats):
        sums = contract_last(weight_ref[m, 0], rows)
        for k in range(top):
            part = (sums * mask[k : k + 1]).astype(BF16)
            for q in range(nx):
                piece = part[:, q * share : (q + 1) * share]

                @pl.when(expert == 0)
                def _():
                    out_ref[q, m * top + k] = piece

                @pl.when(expert > 0)
                def _():
                    out_ref[q, m * top + k] += piece


def pick(weights, everything, mask, place, rows, nx):
    mats, experts, units, width = weights.shape
    top, total = mask.shape[1:]
    ny = everything.shape[0]
    return pl.pallas_call(
        functools.partial(pick_kernel, mats, top, nx),
        grid=(experts,),
        in_specs=[
            pl.BlockSpec((mats, 1, units, width), lambda e: (0, e, 0, 0)),
            pl.BlockSpec((ny, rows, width), lambda e: (0, place, 0)),
            pl.BlockSpec((1, top, total), lambda e: (e, 0, 0)),
        ],
        out_specs=pl.BlockSpec((nx, mats * top, units, total // nx), lambda e: (0, 0, 0, 0)),
        out_shape=jax.ShapeDtypeStruct((nx, mats * top, units, total // nx), BF16),
        compiler_params=pltpu.CompilerParams(vmem_limit_bytes=VMEM_BYTES),
        cost_estimate=pl.CostEstimate(
            flops=2 * mats * experts * units * width * total,
            bytes_accessed=2 * (weights.size + total * width + mats * top * units * total),
            transcendentals=0,
        ),
        name="pick",
    )(weights, everything, mask)


def output_kernel(mats, top, nx, split, shared_ref, weight_ref, mask_ref, wide_ref, out_ref, acc_ref):
    expert = pl.program_id(0)
    mask = mask_ref[0]
    share = shared_ref.shape[3]
    product = None
    for m in range(mats):
        pieces = []
        for q in range(nx):
            piece = None
            for k in range(top):
                value = shared_ref[q, m * top + k].astype(F32)
                term = value * mask[k : k + 1, q * share : (q + 1) * share]
                piece = term if piece is None else piece + term
            pieces.append(piece.astype(BF16))
        wide = jnp.concatenate(pieces, axis=1)
        wide_ref[m, 0] = wide
        term = contract_first(wide, weight_ref[m, 0])
        product = term if product is None else product + term

    @pl.when(expert == 0)
    def _():
        acc_ref[...] = product

    @pl.when(expert > 0)
    def _():
        acc_ref[...] += product

    @pl.when(expert == pl.num_programs(0) - 1)
    def _():
        total = acc_ref[...].astype(BF16)
        if split is None:
            out_ref[...] = total
        else:
            ny, nh = split
            blocks = total.reshape(ny, nh, total.shape[0] // (ny * nh), total.shape[1])
            for h in range(nh):
                out_ref[h] = blocks[:, h]


def output(shared, weights, mask, split):
    mats, experts, units, width = weights.shape
    top, total = mask.shape[1:]
    nx, _, _, share = shared.shape
    if split is None:
        shape = (total, width)
    else:
        shape = (split[1], split[0], total // (split[0] * split[1]), width)
    return pl.pallas_call(
        functools.partial(output_kernel, mats, top, nx, split),
        grid=(experts,),
        in_specs=[
            pl.BlockSpec(shared.shape, lambda e: (0, 0, 0, 0)),
            pl.BlockSpec((mats, 1, units, width), lambda e: (0, e, 0, 0)),
            pl.BlockSpec((1, top, total), lambda e: (e, 0, 0)),
        ],
        out_specs=[
            pl.BlockSpec((mats, 1, units, total), lambda e: (0, e, 0, 0)),
            pl.BlockSpec(shape, lambda e: (0,) * len(shape)),
        ],
        out_shape=[
            jax.ShapeDtypeStruct((mats, experts, units, total), BF16),
            jax.ShapeDtypeStruct(shape, BF16),
        ],
        scratch_shapes=[pltpu.VMEM((total, width), F32)],
        compiler_params=pltpu.CompilerParams(vmem_limit_bytes=VMEM_BYTES),
        cost_estimate=pl.CostEstimate(
            flops=2 * mats * experts * units * width * total,
            bytes_accessed=2 * (weights.size + total * width + 2 * shared.size),
            transcendentals=0,
        ),
        name="output",
    )(shared, weights, mask)


def body(tokens, slot_ids, gate_values, slot_expert, w_gate, w_up, w_down, cotangent):
    block, width = tokens.shape
    experts, units, _ = w_gate.shape
    ny, nh, nl, nx = (lax.axis_size(a) for a in ("y", "zh", "zl", "x"))
    top = slot_ids.shape[1]
    rows = block // nl
    total = ny * rows
    share = total // nx
    many = 2 * nl * units

    def own_rows(value):
        return lax.dynamic_slice_in_dim(value, lax.axis_index("zl") * rows, rows, axis=0)

    ids, values = own_rows(slot_ids), own_rows(gate_values)
    numbers = jnp.arange(slot_expert.shape[0], dtype=jnp.int32)
    chosen = jnp.sum(
        jnp.where(ids[:, :, None] == numbers, slot_expert[None, None, :], 0), axis=-1
    ).astype(F32)
    part0 = short(values)
    part1 = short(values - part0)
    part2 = short(values - part0 - part1)
    meta = jnp.stack([chosen, part0, part1, part2]).transpose(0, 2, 1).astype(BF16)
    facts_of = 4 * top * rows
    meta = jnp.pad(meta.reshape(1, facts_of), ((0, 15), (0, width - facts_of)))
    packed = jnp.concatenate([own_rows(tokens), own_rows(cotangent), meta], axis=0)
    held = packed.shape[0]
    everything = lax.all_gather(packed, "y", axis=0, tiled=True).reshape(ny, held, width)

    own = jnp.stack([w_gate, w_up, w_down])
    near = swap(own, "zl")
    weights = jnp.concatenate([own, swap(own, "core"), near, swap(near, "core")], axis=2)

    facts = everything[:, 2 * rows, :facts_of].reshape(ny, 4, top, rows).astype(F32)
    facts = facts.transpose(1, 2, 0, 3).reshape(4, top, total)
    scale = facts[1] + facts[2] + facts[3]
    mask = (facts[0][None] == jnp.arange(experts, dtype=F32)[:, None, None]).astype(F32)
    own_scale = lax.dynamic_slice_in_dim(scale, lax.axis_index("x") * share, share, axis=1)[:, None]

    def add_up(picked):
        arrived = lax.all_to_all(picked, "x", split_axis=0, concat_axis=0, tiled=True)
        return jnp.sum(arrived.astype(F32), axis=0).reshape(-1, top, many, share)

    gate, up = add_up(pick(weights[:2], everything, mask, 0, rows, nx))
    dh = own_scale * add_up(pick(weights[2:], everything, mask, 1, rows, nx))[0]
    sg = jax.nn.sigmoid(gate)
    active = gate * sg
    hidden = (own_scale * (active * up)).astype(BF16)
    dgate = (dh * up * sg * (1.0 + gate * (1.0 - sg))).astype(BF16)
    dup = (dh * active).astype(BF16)
    hidden_all = spread(hidden, "x", nx)
    grads_all = spread(jnp.concatenate([dgate, dup]), "x", nx)

    hidden_wide, mixed_part = output(hidden_all, weights[2:], mask, (ny, nh))
    grads_wide, back_part = output(grads_all, weights[:2], mask, None)

    small = rows // nh
    mixed = lax.all_to_all(mixed_part, "zh", split_axis=0, concat_axis=0, tiled=True)
    mixed = jnp.sum(mixed.astype(F32), axis=0).astype(BF16)
    mixed = lax.all_to_all(mixed, "y", split_axis=0, concat_axis=0, tiled=True)
    mixed = jnp.sum(mixed.astype(F32), axis=0).astype(BF16)

    back = lax.psum_scatter(back_part, "y", scatter_dimension=0, tiled=True)
    back = back.reshape(nh, small, width)
    back = lax.all_to_all(back, "zh", split_axis=0, concat_axis=0, tiled=True)
    back = jnp.sum(back.astype(F32), axis=0).astype(BF16)

    def finish(piece):
        pieces = spread(piece, ("zh", "zl"), nh * nl).reshape(nh, nl, small, width)
        return pieces.transpose(1, 0, 2, 3).reshape(block, width)

    def weight_gradient(wide, values):
        part = jnp.dot(wide.reshape(-1, total), values, preferred_element_type=F32)
        part = part.astype(BF16).reshape(experts, nl, 2, units, width)
        sent = swap(part[:, :, 1], "core")
        part = part[:, :, 0].astype(F32) + sent.astype(F32)
        sent = swap(part[:, 1].astype(BF16), "zl")
        return (part[:, 0] + sent.astype(F32)).astype(BF16)

    rows_x = everything[:, :rows].reshape(total, width)
    rows_c = everything[:, rows : 2 * rows].reshape(total, width)
    grad_down = weight_gradient(hidden_wide[0], rows_c)
    grad_gate = weight_gradient(grads_wide[0], rows_x)
    grad_up = weight_gradient(grads_wide[1], rows_x)
    return (finish(mixed), finish(back), grad_gate, grad_up, grad_down)


def solution(mesh):
    dp, ep, mp = mesh.shape["dp"], mesh.shape["expert"], mesh.shape["mp"]
    split = Mesh(
        mesh.devices.reshape(dp // 2, 2, ep // 2, 2, mp), ("y", "core", "zh", "zl", "x")
    )
    rows = ("y", "core")
    stored = P(None, ("y", "core", "zh", "zl"), "x")
    return jax.shard_map(
        body,
        mesh=split,
        in_specs=(
            P(rows, "x"),
            P(rows, None),
            P(rows, None),
            P(),
            stored,
            stored,
            stored,
            P(rows, "x"),
        ),
        out_specs=(P(rows, "x"), P(rows, "x"), stored, stored, stored),
        check_vma=False,
    )
```

```python
import functools
import jax
import jax.numpy as jnp
from jax import lax
from jax.experimental import pallas as pl
from jax.experimental.pallas import tpu as pltpu
from jax.sharding import Mesh, PartitionSpec as P

F32 = jnp.float32
BF16 = jnp.bfloat16
VMEM_BYTES = 48 * 1024 * 1024


def short(value):
    return lax.reduce_precision(value, exponent_bits=8, mantissa_bits=7)


def swap(value, axis):
    return lax.ppermute(value, axis, [(0, 1), (1, 0)])


def contract_last(left, right):
    return lax.dot_general(left, right, (((1,), (1,)), ((), ())), preferred_element_type=F32)


def contract_first(left, right):
    return lax.dot_general(left, right, (((0,), (0,)), ((), ())), preferred_element_type=F32)


def spread(value, axis, count):
    copies = jnp.broadcast_to(value[None], (count,) + value.shape)
    copies = lax.optimization_barrier(copies)
    return lax.all_to_all(copies, axis, split_axis=0, concat_axis=0, tiled=True)


def pick_kernel(top, nx, experts, weight_ref, rows_ref, cots_ref, mask_ref, out_ref):
    width = rows_ref.shape[2]
    mats, parts, stored = weight_ref.shape[:3]
    units = stored // experts
    share = out_ref.shape[3]
    for m in range(mats):
        rows = (cots_ref if m == mats - 1 else rows_ref)[...].reshape(-1, width)
        picked = [[] for _ in range(top)]
        for p in range(parts):
            sums = contract_last(weight_ref[m, p], rows)
            for k in range(top):
                value = None
                for e in range(experts):
                    term = sums[e * units : (e + 1) * units] * mask_ref[e, k : k + 1]
                    value = term if value is None else value + term
                picked[k].append(value)
        for k in range(top):
            value = jnp.concatenate(picked[k], axis=0).astype(BF16)
            for q in range(nx):
                out_ref[q, m * top + k] = value[:, q * share : (q + 1) * share]


def pick(weights, experts, everything, mask, rows, nx):
    mats, parts, stored, width = weights.shape
    top, total = mask.shape[1:]
    ny = everything.shape[0]
    many = parts * stored // experts
    pieces = (nx, mats * top, many, total // nx)
    return pl.pallas_call(
        functools.partial(pick_kernel, top, nx, experts),
        grid=(1,),
        in_specs=[
            pl.BlockSpec(weights.shape, lambda i: (0, 0, 0, 0)),
            pl.BlockSpec((ny, rows, width), lambda i: (0, 0, 0)),
            pl.BlockSpec((ny, rows, width), lambda i: (0, 1, 0)),
            pl.BlockSpec((experts, top, total), lambda i: (0, 0, 0)),
        ],
        out_specs=pl.BlockSpec(pieces, lambda i: (0, 0, 0, 0)),
        out_shape=jax.ShapeDtypeStruct(pieces, BF16),
        compiler_params=pltpu.CompilerParams(vmem_limit_bytes=VMEM_BYTES),
        cost_estimate=pl.CostEstimate(
            flops=2 * mats * parts * stored * width * total,
            bytes_accessed=2 * mats * (parts * stored * width + top * many * total)
            + 4 * total * width,
            transcendentals=0,
        ),
        name="pick",
    )(weights, everything, everything, mask)


def middle_kernel(top, arrived_ref, scale_ref, out_ref):
    nx = arrived_ref.shape[0]

    def add_up(which):
        value = arrived_ref[0, which].astype(F32)
        for q in range(1, nx):
            value = value + arrived_ref[q, which].astype(F32)
        return value

    for k in range(top):
        scale = scale_ref[k : k + 1]
        gate, up, dh = add_up(k), add_up(top + k), scale * add_up(2 * top + k)
        sg = jax.nn.sigmoid(gate)
        active = gate * sg
        dgate = (dh * up * sg * (1.0 + gate * (1.0 - sg))).astype(BF16)
        dup = (dh * active).astype(BF16)
        hidden = (scale * (active * up)).astype(BF16)
        for q in range(nx):
            out_ref[q, k] = dgate
            out_ref[q, top + k] = dup
            out_ref[q, 2 * top + k] = hidden


def middle(arrived, scale):
    return pl.pallas_call(
        functools.partial(middle_kernel, scale.shape[0]),
        out_shape=jax.ShapeDtypeStruct(arrived.shape, BF16),
        compiler_params=pltpu.CompilerParams(vmem_limit_bytes=VMEM_BYTES),
        cost_estimate=pl.CostEstimate(
            flops=6 * arrived.size, bytes_accessed=4 * arrived.size, transcendentals=arrived.size
        ),
        name="middle",
    )(arrived, scale)


def output_kernel(top, nx, experts, shared_ref, weight_ref, mask_ref, wide_ref, out_ref):
    share = shared_ref.shape[3]
    mats, parts, stored = weight_ref.shape[:3]
    units = stored // experts
    ny, _, rows, width = out_ref.shape
    for m in range(mats):
        values = [
            [shared_ref[q, m * top + k].astype(F32) for k in range(top)] for q in range(nx)
        ]
        for p in range(parts):
            pieces = []
            for e in range(experts):
                line = []
                for q in range(nx):
                    piece = None
                    for k in range(top):
                        value = values[q][k][p * units : (p + 1) * units]
                        term = value * mask_ref[e, k : k + 1, q * share : (q + 1) * share]
                        piece = term if piece is None else piece + term
                    line.append(piece)
                pieces.append(jnp.concatenate(line, axis=1))
            wide_ref[p, m] = jnp.concatenate(pieces, axis=0).astype(BF16)
    for which, members in ((0, range(mats - 1, mats)), (1, range(mats - 1))):
        product = None
        for m in members:
            for p in range(parts):
                term = contract_first(wide_ref[p, m], weight_ref[m, p])
                product = term if product is None else product + term
        out_ref[:, which] = product.astype(BF16).reshape(ny, rows, width)


def output(shared, weights, experts, mask, ny):
    mats, parts, stored, width = weights.shape
    top, total = mask.shape[1:]
    nx = shared.shape[0]
    both = (ny, 2, total // ny, width)
    wide = (parts, mats, stored, total)
    return pl.pallas_call(
        functools.partial(output_kernel, top, nx, experts),
        grid=(1,),
        in_specs=[
            pl.BlockSpec(shared.shape, lambda i: (0, 0, 0, 0)),
            pl.BlockSpec(weights.shape, lambda i: (0, 0, 0, 0)),
            pl.BlockSpec((experts, top, total), lambda i: (0, 0, 0)),
        ],
        out_specs=[
            pl.BlockSpec(wide, lambda i: (0, 0, 0, 0)),
            pl.BlockSpec(both, lambda i: (0, 0, 0, 0)),
        ],
        out_shape=[jax.ShapeDtypeStruct(wide, BF16), jax.ShapeDtypeStruct(both, BF16)],
        compiler_params=pltpu.CompilerParams(vmem_limit_bytes=VMEM_BYTES),
        cost_estimate=pl.CostEstimate(
            flops=2 * mats * parts * stored * width * total,
            bytes_accessed=2 * (mats * parts * stored * (width + total) + 2 * total * width),
            transcendentals=0,
        ),
        name="output",
    )(shared, weights, mask)


def body(tokens, slot_ids, gate_values, slot_expert, w_gate, w_up, w_down, cotangent):
    block, width = tokens.shape
    experts, units, _ = w_gate.shape
    ny, nh, nl, nx = (lax.axis_size(a) for a in ("y", "zh", "zl", "x"))
    top = slot_ids.shape[1]
    rows = block // nl
    total = ny * rows
    share = total // nx
    many = 2 * nl * units
    stored = experts * units

    def own_rows(value):
        return lax.dynamic_slice_in_dim(value, lax.axis_index("zl") * rows, rows, axis=0)

    ids, values = own_rows(slot_ids), own_rows(gate_values)
    numbers = jnp.arange(slot_expert.shape[0], dtype=jnp.int32)
    chosen = jnp.sum(
        jnp.where(ids[:, :, None] == numbers, slot_expert[None, None, :], 0), axis=-1
    ).astype(F32)
    part0 = short(values)
    part1 = short(values - part0)
    part2 = short(values - part0 - part1)
    meta = jnp.stack([chosen, part0, part1, part2]).transpose(0, 2, 1).astype(BF16)
    facts_of = 4 * top * rows
    meta = jnp.pad(meta.reshape(1, facts_of), ((0, 15), (0, width - facts_of)))
    packed = jnp.concatenate([own_rows(tokens), own_rows(cotangent), meta], axis=0)
    held = packed.shape[0]
    everything = lax.all_gather(packed, "y", axis=0, tiled=True).reshape(ny, held, width)

    own = jnp.stack([w_gate, w_up, w_down]).reshape(3, 1, stored, width)
    near = swap(own, "zl")
    weights = jnp.concatenate([own, near, swap(own, "core"), swap(near, "core")], axis=1)
    everything, weights = lax.optimization_barrier((everything, weights))

    facts = everything[:, 2 * rows, :facts_of].reshape(ny, 4, top, rows).astype(F32)
    facts = facts.transpose(1, 2, 0, 3).reshape(4, top, total)
    scale = facts[1] + facts[2] + facts[3]
    mask = (facts[0][None] == jnp.arange(experts, dtype=F32)[:, None, None]).astype(F32)
    own_scale = lax.dynamic_slice_in_dim(scale, lax.axis_index("x") * share, share, axis=1)

    def exchange(value):
        return lax.all_to_all(value, "x", split_axis=0, concat_axis=0, tiled=True)

    picked = pick(weights, experts, everything, mask, rows, nx)
    shared = exchange(middle(exchange(picked), own_scale))
    wide, parts = output(shared, weights, experts, mask, ny)
    small = rows // nh
    parts = lax.psum_scatter(
        parts.reshape(ny * 2 * rows, width), "y", scatter_dimension=0, tiled=True
    )

    rows_x = everything[:, :rows].reshape(total, width)
    rows_c = everything[:, rows : 2 * rows].reshape(total, width)

    def products(wide):
        groups = ((wide[:, :2], rows_x), (wide[:, 2:], rows_c))
        return [
            jnp.dot(left.reshape(-1, total), right, preferred_element_type=F32).reshape(
                nl, -1, stored, width
            )
            for left, right in groups
        ]

    sent = [swap(value.astype(BF16), "core").astype(F32) for value in products(wide[nl:])]
    kept = products(wide[:nl])
    near = [swap((a[1] + b[1]).astype(BF16), "zl") for a, b in zip(kept, sent)]
    parts, near[0], near[1] = lax.optimization_barrier((parts, near[0], near[1]))
    done = [
        (a[0] + b[0] + c.astype(F32)).astype(BF16).reshape(-1, experts, units, width)
        for a, b, c in zip(kept, sent, near)
    ]

    parts = parts.reshape(2, nh, small, width).transpose(1, 0, 2, 3)
    parts = lax.all_to_all(parts, "zh", split_axis=0, concat_axis=0, tiled=True)
    parts = jnp.sum(parts.astype(F32), axis=0).astype(BF16)
    ends = spread(parts, ("zh", "zl"), nh * nl)
    ends = ends.reshape(nh, nl, 2, small, width).transpose(2, 1, 0, 3, 4).reshape(2, block, width)
    return (ends[0], ends[1], done[0][0], done[0][1], done[1][0])


def solution(mesh):
    dp, ep, mp = mesh.shape["dp"], mesh.shape["expert"], mesh.shape["mp"]
    split = Mesh(
        mesh.devices.reshape(dp // 2, 2, ep // 2, 2, mp), ("y", "core", "zh", "zl", "x")
    )
    rows = ("y", "core")
    stored = P(None, ("y", "core", "zh", "zl"), "x")
    return jax.shard_map(
        body,
        mesh=split,
        in_specs=(
            P(rows, "x"),
            P(rows, None),
            P(rows, None),
            P(),
            stored,
            stored,
            stored,
            P(rows, "x"),
        ),
        out_specs=(P(rows, "x"), P(rows, "x"), stored, stored, stored),
        check_vma=False,
    )
```

```python
import functools
import jax
import jax.numpy as jnp
from jax import lax
from jax.experimental import pallas as pl
from jax.experimental.pallas import tpu as pltpu
from jax.sharding import Mesh, PartitionSpec as P

F32 = jnp.float32
BF16 = jnp.bfloat16
VMEM_BYTES = 24 * 1024 * 1024


def short(value):
    return lax.reduce_precision(value, exponent_bits=8, mantissa_bits=7)


def swap(value, axis):
    return lax.ppermute(value, axis, [(0, 1), (1, 0)])


def contract_last(left, right):
    return lax.dot_general(left, right, (((1,), (1,)), ((), ())), preferred_element_type=F32)


def contract_first(left, right):
    return lax.dot_general(left, right, (((0,), (0,)), ((), ())), preferred_element_type=F32)


def spread(value, axis, count):
    copies = jnp.broadcast_to(value[None], (count,) + value.shape)
    copies = lax.optimization_barrier(copies)
    return lax.all_to_all(copies, axis, split_axis=0, concat_axis=0, tiled=True)


def pick_kernel(experts, *refs):
    *weight_refs, rows_ref, mask_ref, out_ref = refs
    rows = rows_ref[...].reshape(-1, rows_ref.shape[2])
    units = weight_refs[0].shape[1] // experts
    nx, top, _, share = out_ref.shape
    picked = [[] for _ in range(top)]
    for weight_ref in weight_refs:
        sums = contract_last(weight_ref[0], rows)
        for k in range(top):
            value = None
            for e in range(experts):
                term = sums[e * units : (e + 1) * units] * mask_ref[e, k : k + 1]
                value = term if value is None else value + term
            picked[k].append(value)
    for k in range(top):
        value = jnp.concatenate(picked[k], axis=0).astype(BF16)
        for q in range(nx):
            out_ref[q, k] = value[:, q * share : (q + 1) * share]


def pick(weights, experts, everything, mask, rows, nx):
    parts = len(weights)
    mats, stored, width = weights[0].shape
    top, total = mask.shape[1:]
    ny = everything.shape[0]
    many = parts * stored // experts
    return pl.pallas_call(
        functools.partial(pick_kernel, experts),
        grid=(mats,),
        in_specs=[pl.BlockSpec((1, stored, width), lambda m: (m, 0, 0))] * parts
        + [
            pl.BlockSpec((ny, rows, width), lambda m: (0, m // (mats - 1), 0)),
            pl.BlockSpec((experts, top, total), lambda m: (0, 0, 0)),
        ],
        out_specs=pl.BlockSpec((nx, top, many, total // nx), lambda m: (0, m, 0, 0)),
        out_shape=jax.ShapeDtypeStruct((nx, mats * top, many, total // nx), BF16),
        compiler_params=pltpu.CompilerParams(vmem_limit_bytes=VMEM_BYTES),
        cost_estimate=pl.CostEstimate(
            flops=2 * mats * parts * stored * width * total,
            bytes_accessed=2 * mats * (parts * stored * width + top * many * total)
            + 4 * total * width,
            transcendentals=0,
        ),
        name="pick",
    )(*weights, everything, mask)


def middle_kernel(top, arrived_ref, scale_ref, out_ref):
    nx = arrived_ref.shape[0]

    def add_up(which):
        value = arrived_ref[0, which].astype(F32)
        for q in range(1, nx):
            value = value + arrived_ref[q, which].astype(F32)
        return value

    for k in range(top):
        scale = scale_ref[k : k + 1]
        gate, up, dh = add_up(k), add_up(top + k), scale * add_up(2 * top + k)
        sg = jax.nn.sigmoid(gate)
        active = gate * sg
        dgate = (dh * up * sg * (1.0 + gate * (1.0 - sg))).astype(BF16)
        dup = (dh * active).astype(BF16)
        hidden = (scale * (active * up)).astype(BF16)
        for q in range(nx):
            out_ref[q, k] = dgate
            out_ref[q, top + k] = dup
            out_ref[q, 2 * top + k] = hidden


def middle(arrived, scale):
    return pl.pallas_call(
        functools.partial(middle_kernel, scale.shape[0]),
        out_shape=jax.ShapeDtypeStruct(arrived.shape, BF16),
        compiler_params=pltpu.CompilerParams(vmem_limit_bytes=VMEM_BYTES),
        cost_estimate=pl.CostEstimate(
            flops=6 * arrived.size, bytes_accessed=4 * arrived.size, transcendentals=arrived.size
        ),
        name="middle",
    )(arrived, scale)


def output_kernel(experts, parts, *refs):
    weight_refs = refs[:parts]
    shared_ref, mask_ref, kept_ref, sent_ref, out_ref, sum_ref = refs[parts:]
    step = pl.program_id(0)
    nx, top, _, share = shared_ref.shape
    units = weight_refs[0].shape[1] // experts
    ny, nh, _, small, width = out_ref.shape
    values = [[shared_ref[q, k].astype(F32) for k in range(top)] for q in range(nx)]
    product = None
    for p in range(parts):
        pieces = []
        for e in range(experts):
            line = []
            for q in range(nx):
                piece = None
                for k in range(top):
                    value = values[q][k][p * units : (p + 1) * units]
                    term = value * mask_ref[e, k : k + 1, q * share : (q + 1) * share]
                    piece = term if piece is None else piece + term
                line.append(piece)
            pieces.append(jnp.concatenate(line, axis=1))
        wide = jnp.concatenate(pieces, axis=0).astype(BF16)
        if p < parts // 2:
            kept_ref[p, 0] = wide
        else:
            sent_ref[p - parts // 2, 0] = wide
        term = contract_first(wide, weight_refs[p][0])
        product = term if product is None else product + term

    @pl.when(step == 0)
    def _():
        out_ref[:, :, 0] = product.astype(BF16).reshape(ny, nh, small, width)

    @pl.when(step == 1)
    def _():
        sum_ref[...] = product

    @pl.when(step == 2)
    def _():
        total = (sum_ref[...] + product).astype(BF16)
        out_ref[:, :, 0] = total.reshape(ny, nh, small, width)


def output(shared, weights, experts, mask, ny, nh):
    parts = len(weights)
    mats, stored, width = weights[0].shape
    top, total = mask.shape[1:]
    nx, _, many, share = shared.shape
    small = total // (ny * nh)

    def matrix(step):
        return lax.rem(step + mats - 1, mats)

    return pl.pallas_call(
        functools.partial(output_kernel, experts, parts),
        grid=(mats,),
        in_specs=[pl.BlockSpec((1, stored, width), lambda i: (matrix(i), 0, 0))] * parts
        + [
            pl.BlockSpec((nx, top, many, share), lambda i: (0, matrix(i), 0, 0)),
            pl.BlockSpec((experts, top, total), lambda i: (0, 0, 0)),
        ],
        out_specs=[
            pl.BlockSpec((parts // 2, 1, stored, total), lambda i: (0, matrix(i), 0, 0)),
            pl.BlockSpec((parts // 2, 1, stored, total), lambda i: (0, matrix(i), 0, 0)),
            pl.BlockSpec((ny, nh, 1, small, width), lambda i: (0, 0, (i + 1) // 2, 0, 0)),
        ],
        out_shape=[
            jax.ShapeDtypeStruct((parts // 2, mats, stored, total), BF16),
            jax.ShapeDtypeStruct((parts // 2, mats, stored, total), BF16),
            jax.ShapeDtypeStruct((ny, nh, 2, small, width), BF16),
        ],
        scratch_shapes=[pltpu.VMEM((total, width), F32)],
        compiler_params=pltpu.CompilerParams(vmem_limit_bytes=2 * VMEM_BYTES),
        cost_estimate=pl.CostEstimate(
            flops=2 * mats * parts * stored * width * total,
            bytes_accessed=2 * (mats * parts * stored * (width + total) + 2 * total * width),
            transcendentals=0,
        ),
        name="output",
    )(*weights, shared, mask)


def body(tokens, slot_ids, gate_values, slot_expert, w_gate, w_up, w_down, cotangent):
    block, width = tokens.shape
    experts, units, _ = w_gate.shape
    ny, nh, nl, nx = (lax.axis_size(a) for a in ("y", "zh", "zl", "x"))
    top = slot_ids.shape[1]
    rows = block // nl
    total = ny * rows
    share = total // nx
    many = 2 * nl * units
    stored = experts * units

    def own_rows(value):
        return lax.dynamic_slice_in_dim(value, lax.axis_index("zl") * rows, rows, axis=0)

    ids, values = own_rows(slot_ids), own_rows(gate_values)
    numbers = jnp.arange(slot_expert.shape[0], dtype=jnp.int32)
    chosen = jnp.sum(
        jnp.where(ids[:, :, None] == numbers, slot_expert[None, None, :], 0), axis=-1
    ).astype(F32)
    part0 = short(values)
    part1 = short(values - part0)
    part2 = short(values - part0 - part1)
    meta = jnp.stack([chosen, part0, part1, part2]).transpose(0, 2, 1).astype(BF16)
    facts_of = 4 * top * rows
    meta = jnp.pad(meta.reshape(1, facts_of), ((0, 15), (0, width - facts_of)))
    packed = jnp.concatenate([own_rows(tokens), own_rows(cotangent), meta], axis=0)
    held = packed.shape[0]
    everything = lax.all_gather(packed, "y", axis=0, tiled=True).reshape(ny, held, width)

    own = jnp.stack([w_gate, w_up, w_down]).reshape(3, stored, width)
    near = swap(own, "zl")
    weights = [own, near, swap(own, "core"), swap(near, "core")]

    facts = everything[:, 2 * rows, :facts_of].reshape(ny, 4, top, rows).astype(F32)
    facts = facts.transpose(1, 2, 0, 3).reshape(4, top, total)
    scale = facts[1] + facts[2] + facts[3]
    mask = (facts[0][None] == jnp.arange(experts, dtype=F32)[:, None, None]).astype(F32)
    own_scale = lax.dynamic_slice_in_dim(scale, lax.axis_index("x") * share, share, axis=1)

    def exchange(value):
        return lax.all_to_all(value, "x", split_axis=0, concat_axis=0, tiled=True)

    mask, own_scale = lax.optimization_barrier((mask, own_scale))
    picked = pick(weights, experts, everything, mask, rows, nx)
    shared = exchange(middle(exchange(picked), own_scale))
    wide_kept, wide_sent, parts = output(shared, weights, experts, mask, ny, nh)
    small = rows // nh
    parts = lax.psum_scatter(
        parts.reshape(ny * 2 * rows, width), "y", scatter_dimension=0, tiled=True
    )

    rows_x = everything[:, :rows].reshape(total, width)
    rows_c = everything[:, rows : 2 * rows].reshape(total, width)

    def products(wide):
        groups = ((wide[:, :2], rows_x), (wide[:, 2:], rows_c))
        return [
            jnp.dot(left.reshape(-1, total), right, preferred_element_type=F32).reshape(
                nl, -1, stored, width
            )
            for left, right in groups
        ]

    sent = [swap(value.astype(BF16), "core").astype(F32) for value in products(wide_sent)]
    kept = products(wide_kept)
    near = [swap((a[1] + b[1]).astype(BF16), "zl") for a, b in zip(kept, sent)]
    parts, near[0], near[1] = lax.optimization_barrier((parts, near[0], near[1]))
    done = [
        (a[0] + b[0] + c.astype(F32)).astype(BF16).reshape(-1, experts, units, width)
        for a, b, c in zip(kept, sent, near)
    ]

    parts = parts.reshape(nh, 2, small, width)
    parts = lax.all_to_all(parts, "zh", split_axis=0, concat_axis=0, tiled=True)
    parts = jnp.sum(parts.astype(F32), axis=0).astype(BF16)
    ends = spread(parts, ("zh", "zl"), nh * nl)
    ends = ends.reshape(nh, nl, 2, small, width).transpose(2, 1, 0, 3, 4).reshape(2, block, width)
    return (ends[0], ends[1], done[0][0], done[0][1], done[1][0])


def solution(mesh):
    dp, ep, mp = mesh.shape["dp"], mesh.shape["expert"], mesh.shape["mp"]
    split = Mesh(
        mesh.devices.reshape(dp // 2, 2, ep // 2, 2, mp), ("y", "core", "zh", "zl", "x")
    )
    rows = ("y", "core")
    stored = P(None, ("y", "core", "zh", "zl"), "x")
    return jax.shard_map(
        body,
        mesh=split,
        in_specs=(
            P(rows, "x"),
            P(rows, None),
            P(rows, None),
            P(),
            stored,
            stored,
            stored,
            P(rows, "x"),
        ),
        out_specs=(P(rows, "x"), P(rows, "x"), stored, stored, stored),
        check_vma=False,
    )
```

```python
import functools
import jax
import jax.numpy as jnp
from jax import lax
from jax.experimental import pallas as pl
from jax.experimental.pallas import tpu as pltpu
from jax.sharding import Mesh, PartitionSpec as P

F32 = jnp.float32
BF16 = jnp.bfloat16
VMEM_BYTES = 24 * 1024 * 1024


def short(value):
    return lax.reduce_precision(value, exponent_bits=8, mantissa_bits=7)


def swap(value, axis):
    return lax.ppermute(value, axis, [(0, 1), (1, 0)])


def contract_last(left, right):
    return lax.dot_general(left, right, (((1,), (1,)), ((), ())), preferred_element_type=F32)


def contract_first(left, right):
    return lax.dot_general(left, right, (((0,), (0,)), ((), ())), preferred_element_type=F32)


def spread(value, axis, count):
    copies = jnp.broadcast_to(value[None], (count,) + value.shape)
    copies = lax.optimization_barrier(copies)
    return lax.all_to_all(copies, axis, split_axis=0, concat_axis=0, tiled=True)


def whole(memory_space):
    return pl.BlockSpec(memory_space=memory_space)


def rows_of(every_ref, rows_ref, sems, mats):
    matrix = pl.program_id(0)
    rows = rows_ref.shape[2]
    loads = [
        pltpu.make_async_copy(every_ref.at[:, pl.ds(i * rows, rows)], rows_ref.at[i], sems.at[i])
        for i in range(2)
    ]

    @pl.when(matrix == 0)
    def _():
        loads[0].start()
        loads[1].start()
        loads[0].wait()

    @pl.when(matrix == mats - 1)
    def _():
        loads[1].wait()

    return rows_ref[matrix // (mats - 1)].reshape(-1, rows_ref.shape[3])


def rows_scratch(ny, rows, width):
    return [pltpu.VMEM((2, ny, rows, width), BF16), pltpu.SemaphoreType.DMA((2,))]


def pick_kernel(experts, mats, *refs):
    *weight_refs, every_ref, mask_ref, out_ref, rows_ref, sems = refs
    rows = rows_of(every_ref, rows_ref, sems, mats)
    units = weight_refs[0].shape[1] // experts
    nx, top, _, share = out_ref.shape
    picked = [[] for _ in range(top)]
    for weight_ref in weight_refs:
        sums = contract_last(weight_ref[0], rows)
        for k in range(top):
            value = None
            for e in range(experts):
                term = sums[e * units : (e + 1) * units] * mask_ref[e, k : k + 1]
                value = term if value is None else value + term
            picked[k].append(value)
    for k in range(top):
        value = jnp.concatenate(picked[k], axis=0).astype(BF16)
        for q in range(nx):
            out_ref[q, k] = value[:, q * share : (q + 1) * share]


def pick(weights, experts, everything, mask, rows, nx):
    parts = len(weights)
    mats, stored, width = weights[0].shape
    top, total = mask.shape[1:]
    ny = everything.shape[0]
    many = parts * stored // experts
    return pl.pallas_call(
        functools.partial(pick_kernel, experts, mats),
        grid=(mats,),
        in_specs=[pl.BlockSpec((1, stored, width), lambda m: (m, 0, 0))] * parts
        + [whole(pltpu.HBM), pl.BlockSpec((experts, top, total), lambda m: (0, 0, 0))],
        out_specs=pl.BlockSpec((nx, top, many, total // nx), lambda m: (0, m, 0, 0)),
        out_shape=jax.ShapeDtypeStruct((nx, mats * top, many, total // nx), BF16),
        scratch_shapes=rows_scratch(ny, rows, width),
        compiler_params=pltpu.CompilerParams(vmem_limit_bytes=VMEM_BYTES),
        cost_estimate=pl.CostEstimate(
            flops=2 * mats * parts * stored * width * total,
            bytes_accessed=2 * mats * (parts * stored * width + top * many * total)
            + 4 * total * width,
            transcendentals=0,
        ),
        name="pick",
    )(*weights, everything, mask)


def middle_kernel(top, arrived_ref, scale_ref, out_ref):
    nx = arrived_ref.shape[0]

    def add_up(which):
        value = arrived_ref[0, which].astype(F32)
        for q in range(1, nx):
            value = value + arrived_ref[q, which].astype(F32)
        return value

    for k in range(top):
        scale = scale_ref[k : k + 1]
        gate, up, dh = add_up(k), add_up(top + k), scale * add_up(2 * top + k)
        sg = jax.nn.sigmoid(gate)
        active = gate * sg
        dgate = (dh * up * sg * (1.0 + gate * (1.0 - sg))).astype(BF16)
        dup = (dh * active).astype(BF16)
        hidden = (scale * (active * up)).astype(BF16)
        for q in range(nx):
            out_ref[q, k] = dgate
            out_ref[q, top + k] = dup
            out_ref[q, 2 * top + k] = hidden


def middle(arrived, scale):
    return pl.pallas_call(
        functools.partial(middle_kernel, scale.shape[0]),
        out_shape=jax.ShapeDtypeStruct(arrived.shape, BF16),
        compiler_params=pltpu.CompilerParams(vmem_limit_bytes=VMEM_BYTES),
        cost_estimate=pl.CostEstimate(
            flops=6 * arrived.size, bytes_accessed=4 * arrived.size, transcendentals=arrived.size
        ),
        name="middle",
    )(arrived, scale)


def widen(shared_ref, mask_ref, experts, units, part):
    nx, top, _, share = shared_ref.shape
    pieces = []
    for e in range(experts):
        line = []
        for q in range(nx):
            piece = None
            for k in range(top):
                value = shared_ref[q, k].astype(F32)[part * units : (part + 1) * units]
                term = value * mask_ref[e, k : k + 1, q * share : (q + 1) * share]
                piece = term if piece is None else piece + term
            line.append(piece)
        pieces.append(jnp.concatenate(line, axis=1))
    return jnp.concatenate(pieces, axis=0).astype(BF16)


def output_kernel(experts, parts, *refs):
    weight_refs = refs[:parts]
    shared_ref, mask_ref, out_ref, sum_ref = refs[parts:]
    step = pl.program_id(0)
    units = weight_refs[0].shape[1] // experts
    ny, nh, _, small, width = out_ref.shape
    product = None
    for p in range(parts):
        wide = widen(shared_ref, mask_ref, experts, units, p)
        term = contract_first(wide, weight_refs[p][0])
        product = term if product is None else product + term

    @pl.when(step == 0)
    def _():
        out_ref[:, :, 0] = product.astype(BF16).reshape(ny, nh, small, width)

    @pl.when(step == 1)
    def _():
        sum_ref[...] = product

    @pl.when(step == 2)
    def _():
        total = (sum_ref[...] + product).astype(BF16)
        out_ref[:, :, 0] = total.reshape(ny, nh, small, width)


def output(shared, weights, experts, mask, ny, nh):
    parts = len(weights)
    mats, stored, width = weights[0].shape
    top, total = mask.shape[1:]
    nx, _, many, share = shared.shape
    small = total // (ny * nh)

    def matrix(step):
        return lax.rem(step + mats - 1, mats)

    return pl.pallas_call(
        functools.partial(output_kernel, experts, parts),
        grid=(mats,),
        in_specs=[pl.BlockSpec((1, stored, width), lambda i: (matrix(i), 0, 0))] * parts
        + [
            pl.BlockSpec((nx, top, many, share), lambda i: (0, matrix(i), 0, 0)),
            pl.BlockSpec((experts, top, total), lambda i: (0, 0, 0)),
        ],
        out_specs=pl.BlockSpec((ny, nh, 1, small, width), lambda i: (0, 0, (i + 1) // 2, 0, 0)),
        out_shape=jax.ShapeDtypeStruct((ny, nh, 2, small, width), BF16),
        scratch_shapes=[pltpu.VMEM((total, width), F32)],
        compiler_params=pltpu.CompilerParams(vmem_limit_bytes=VMEM_BYTES),
        cost_estimate=pl.CostEstimate(
            flops=2 * mats * parts * stored * width * total,
            bytes_accessed=2 * (mats * parts * stored * width + shared.size + 2 * total * width),
            transcendentals=0,
        ),
        name="output",
    )(*weights, shared, mask)


def gradient_kernel(experts, part, start, shared_ref, mask_ref, every_ref, out_ref, rows_ref, sems):
    rows = rows_ref.shape[1]
    load = pltpu.make_async_copy(every_ref.at[:, pl.ds(start, rows)], rows_ref, sems.at[0])

    @pl.when(pl.program_id(0) == 0)
    def _():
        load.start()
        load.wait()

    values = rows_ref[...].reshape(-1, rows_ref.shape[2])
    units = out_ref.shape[2] // experts
    for p in range(out_ref.shape[0]):
        wide = widen(shared_ref, mask_ref, experts, units, part + p)
        out_ref[p, 0] = jnp.dot(wide, values, preferred_element_type=F32).astype(BF16)


def gradient(shared, mask, everything, first, mats, part, parts, start, units, rows):
    experts, top, total = mask.shape
    nx, _, many, share = shared.shape
    ny, _, width = everything.shape
    stored = experts * units
    return pl.pallas_call(
        functools.partial(gradient_kernel, experts, part, start),
        grid=(mats,),
        in_specs=[
            pl.BlockSpec((nx, top, many, share), lambda m: (0, first + m, 0, 0)),
            pl.BlockSpec((experts, top, total), lambda m: (0, 0, 0)),
            whole(pltpu.HBM),
        ],
        out_specs=pl.BlockSpec((parts, 1, stored, width), lambda m: (0, m, 0, 0)),
        out_shape=jax.ShapeDtypeStruct((parts, mats, stored, width), BF16),
        scratch_shapes=[pltpu.VMEM((ny, rows, width), BF16), pltpu.SemaphoreType.DMA((1,))],
        compiler_params=pltpu.CompilerParams(vmem_limit_bytes=VMEM_BYTES),
        cost_estimate=pl.CostEstimate(
            flops=2 * mats * parts * stored * width * total,
            bytes_accessed=2 * (mats * parts * stored * width + shared.size + total * width),
            transcendentals=0,
        ),
        name="gradient",
    )(shared, mask, everything)


def body(tokens, slot_ids, gate_values, slot_expert, w_gate, w_up, w_down, cotangent):
    block, width = tokens.shape
    experts, units, _ = w_gate.shape
    ny, nh, nl, nx = (lax.axis_size(a) for a in ("y", "zh", "zl", "x"))
    top = slot_ids.shape[1]
    rows = block // nl
    total = ny * rows
    share = total // nx
    many = 2 * nl * units
    stored = experts * units

    def own_rows(value):
        return lax.dynamic_slice_in_dim(value, lax.axis_index("zl") * rows, rows, axis=0)

    ids, values = own_rows(slot_ids), own_rows(gate_values)
    numbers = jnp.arange(slot_expert.shape[0], dtype=jnp.int32)
    chosen = jnp.sum(
        jnp.where(ids[:, :, None] == numbers, slot_expert[None, None, :], 0), axis=-1
    ).astype(F32)
    part0 = short(values)
    part1 = short(values - part0)
    part2 = short(values - part0 - part1)
    meta = jnp.stack([chosen, part0, part1, part2]).transpose(0, 2, 1).astype(BF16)
    facts_of = 4 * top * rows
    meta = jnp.pad(meta.reshape(1, facts_of), ((0, 15), (0, width - facts_of)))
    packed = jnp.concatenate([own_rows(tokens), own_rows(cotangent), meta], axis=0)
    held = packed.shape[0]
    everything = lax.all_gather(packed, "y", axis=0, tiled=True).reshape(ny, held, width)

    own = jnp.stack([w_gate, w_up, w_down]).reshape(3, stored, width)
    near = swap(own, "zl")
    weights = [own, near, swap(own, "core"), swap(near, "core")]

    facts = everything[:, 2 * rows, :facts_of].reshape(ny, 4, top, rows).astype(F32)
    facts = facts.transpose(1, 2, 0, 3).reshape(4, top, total)
    scale = facts[1] + facts[2] + facts[3]
    mask = (facts[0][None] == jnp.arange(experts, dtype=F32)[:, None, None]).astype(F32)
    own_scale = lax.dynamic_slice_in_dim(scale, lax.axis_index("x") * share, share, axis=1)

    def exchange(value):
        return lax.all_to_all(value, "x", split_axis=0, concat_axis=0, tiled=True)

    mask, own_scale = lax.optimization_barrier((mask, own_scale))
    picked = pick(weights, experts, everything, mask, rows, nx)
    shared = exchange(middle(exchange(picked), own_scale))
    parts = output(shared, weights, experts, mask, ny, nh)
    small = rows // nh
    parts, shared = lax.optimization_barrier((parts, shared))
    scattered = lax.psum_scatter(
        parts.reshape(ny * 2 * rows, width), "y", scatter_dimension=0, tiled=True
    )

    def product(first, mats, part):
        start = rows if first == 2 else 0
        return gradient(shared, mask, everything, first, mats, part, nl, start, units, rows)

    def near_of(kept, sent):
        return swap((kept[1].astype(F32) + sent[1].astype(F32)).astype(BF16), "zl")

    sent_down = product(2, 1, nl)
    sent_down, shared = lax.optimization_barrier((sent_down, shared))
    sent_down = swap(sent_down, "core")
    sent = product(0, 2, nl)
    sent, shared = lax.optimization_barrier((sent, shared))
    sent = swap(sent, "core")
    kept_down = product(2, 1, 0)
    near_down = near_of(kept_down, sent_down)
    kept = product(0, 2, 0)
    near = near_of(kept, sent)

    parts = scattered.reshape(nh, 2, small, width)
    parts = lax.all_to_all(parts, "zh", split_axis=0, concat_axis=0, tiled=True)
    parts = jnp.sum(parts.astype(F32), axis=0).astype(BF16)
    parts, near_down, near = lax.optimization_barrier((parts, near_down, near))
    ends = spread(parts, ("zh", "zl"), nh * nl)
    ends = ends.reshape(nh, nl, 2, small, width).transpose(2, 1, 0, 3, 4).reshape(2, block, width)

    def finish(kept, sent, near):
        done = sum(value.astype(F32) for value in (kept[0], sent[0], near)).astype(BF16)
        return done.reshape(-1, experts, units, width)

    (grad_down,) = finish(kept_down, sent_down, near_down)
    grad_gate, grad_up = finish(kept, sent, near)

    return (ends[0], ends[1], grad_gate, grad_up, grad_down)


def solution(mesh):
    dp, ep, mp = mesh.shape["dp"], mesh.shape["expert"], mesh.shape["mp"]
    split = Mesh(
        mesh.devices.reshape(dp // 2, 2, ep // 2, 2, mp), ("y", "core", "zh", "zl", "x")
    )
    rows = ("y", "core")
    stored = P(None, ("y", "core", "zh", "zl"), "x")
    return jax.shard_map(
        body,
        mesh=split,
        in_specs=(
            P(rows, "x"),
            P(rows, None),
            P(rows, None),
            P(),
            stored,
            stored,
            stored,
            P(rows, "x"),
        ),
        out_specs=(P(rows, "x"), P(rows, "x"), stored, stored, stored),
        check_vma=False,
    )
```

```python
import functools
import jax
import jax.numpy as jnp
from jax import lax
from jax.experimental import pallas as pl
from jax.experimental.pallas import tpu as pltpu
from jax.sharding import Mesh, PartitionSpec as P

F32 = jnp.float32
BF16 = jnp.bfloat16
VMEM_BYTES = 24 * 1024 * 1024


def short(value):
    return lax.reduce_precision(value, exponent_bits=8, mantissa_bits=7)


def swap(value, axis):
    return lax.ppermute(value, axis, [(0, 1), (1, 0)])


def contract_last(left, right):
    return lax.dot_general(left, right, (((1,), (1,)), ((), ())), preferred_element_type=F32)


def contract_first(left, right):
    return lax.dot_general(left, right, (((0,), (0,)), ((), ())), preferred_element_type=F32)


def whole(memory_space):
    return pl.BlockSpec(memory_space=memory_space)


def rows_of(every_ref, rows_ref, sems, mats):
    matrix = pl.program_id(0)
    rows = rows_ref.shape[2]
    loads = [
        pltpu.make_async_copy(every_ref.at[:, pl.ds(i * rows, rows)], rows_ref.at[i], sems.at[i])
        for i in range(2)
    ]

    @pl.when(matrix == 0)
    def _():
        loads[0].start()
        loads[1].start()
        loads[0].wait()

    @pl.when(matrix == mats - 1)
    def _():
        loads[1].wait()

    return rows_ref[matrix // (mats - 1)].reshape(-1, rows_ref.shape[3])


def rows_scratch(ny, rows, width):
    return [pltpu.VMEM((2, ny, rows, width), BF16), pltpu.SemaphoreType.DMA((2,))]


def pick_kernel(experts, mats, *refs):
    *weight_refs, every_ref, mask_ref, out_ref, rows_ref, sems = refs
    rows = rows_of(every_ref, rows_ref, sems, mats)
    units = weight_refs[0].shape[1] // experts
    nx, top, _, share = out_ref.shape
    picked = [[] for _ in range(top)]
    for weight_ref in weight_refs:
        sums = contract_last(weight_ref[0], rows)
        for k in range(top):
            value = None
            for e in range(experts):
                term = sums[e * units : (e + 1) * units] * mask_ref[e, k : k + 1]
                value = term if value is None else value + term
            picked[k].append(value)
    for k in range(top):
        value = jnp.concatenate(picked[k], axis=0).astype(BF16)
        for q in range(nx):
            out_ref[q, k] = value[:, q * share : (q + 1) * share]


def pick(weights, experts, everything, mask, rows, nx):
    parts = len(weights)
    mats, stored, width = weights[0].shape
    top, total = mask.shape[1:]
    ny = everything.shape[0]
    many = parts * stored // experts
    return pl.pallas_call(
        functools.partial(pick_kernel, experts, mats),
        grid=(mats,),
        in_specs=[pl.BlockSpec((1, stored, width), lambda m: (m, 0, 0))] * parts
        + [whole(pltpu.HBM), pl.BlockSpec((experts, top, total), lambda m: (0, 0, 0))],
        out_specs=pl.BlockSpec((nx, top, many, total // nx), lambda m: (0, m, 0, 0)),
        out_shape=jax.ShapeDtypeStruct((nx, mats * top, many, total // nx), BF16),
        scratch_shapes=rows_scratch(ny, rows, width),
        compiler_params=pltpu.CompilerParams(vmem_limit_bytes=VMEM_BYTES),
        cost_estimate=pl.CostEstimate(
            flops=2 * mats * parts * stored * width * total,
            bytes_accessed=2 * mats * (parts * stored * width + top * many * total)
            + 4 * total * width,
            transcendentals=0,
        ),
        name="pick",
    )(*weights, everything, mask)


def middle_kernel(top, arrived_ref, scale_ref, out_ref):
    nx = arrived_ref.shape[0]

    def add_up(which):
        value = arrived_ref[0, which].astype(F32)
        for q in range(1, nx):
            value = value + arrived_ref[q, which].astype(F32)
        return value

    for k in range(top):
        scale = scale_ref[k : k + 1]
        gate, up, dh = add_up(k), add_up(top + k), scale * add_up(2 * top + k)
        sg = jax.nn.sigmoid(gate)
        active = gate * sg
        dgate = (dh * up * sg * (1.0 + gate * (1.0 - sg))).astype(BF16)
        dup = (dh * active).astype(BF16)
        hidden = (scale * (active * up)).astype(BF16)
        for q in range(nx):
            out_ref[q, k] = dgate
            out_ref[q, top + k] = dup
            out_ref[q, 2 * top + k] = hidden


def middle(arrived, scale):
    return pl.pallas_call(
        functools.partial(middle_kernel, scale.shape[0]),
        out_shape=jax.ShapeDtypeStruct(arrived.shape, BF16),
        compiler_params=pltpu.CompilerParams(vmem_limit_bytes=VMEM_BYTES),
        cost_estimate=pl.CostEstimate(
            flops=6 * arrived.size, bytes_accessed=4 * arrived.size, transcendentals=arrived.size
        ),
        name="middle",
    )(arrived, scale)


def widen(shared_ref, mask_ref, experts, units, part):
    nx, top, _, share = shared_ref.shape
    pieces = []
    for e in range(experts):
        line = []
        for q in range(nx):
            piece = None
            for k in range(top):
                value = shared_ref[q, k].astype(F32)[part * units : (part + 1) * units]
                term = value * mask_ref[e, k : k + 1, q * share : (q + 1) * share]
                piece = term if piece is None else piece + term
            line.append(piece)
        pieces.append(jnp.concatenate(line, axis=1))
    return jnp.concatenate(pieces, axis=0).astype(BF16)


def output_kernel(experts, parts, *refs):
    weight_refs = refs[:parts]
    shared_ref, mask_ref, out_ref, sum_ref = refs[parts:]
    step = pl.program_id(0)
    units = weight_refs[0].shape[1] // experts
    ny, nh, _, small, width = out_ref.shape
    product = None
    for p in range(parts):
        wide = widen(shared_ref, mask_ref, experts, units, p)
        term = contract_first(wide, weight_refs[p][0])
        product = term if product is None else product + term

    @pl.when(step == 0)
    def _():
        out_ref[:, :, 0] = product.astype(BF16).reshape(ny, nh, small, width)

    @pl.when(step == 1)
    def _():
        sum_ref[...] = product

    @pl.when(step == 2)
    def _():
        total = (sum_ref[...] + product).astype(BF16)
        out_ref[:, :, 0] = total.reshape(ny, nh, small, width)


def output(shared, weights, experts, mask, ny, nh):
    parts = len(weights)
    mats, stored, width = weights[0].shape
    top, total = mask.shape[1:]
    nx, _, many, share = shared.shape
    small = total // (ny * nh)

    def matrix(step):
        return lax.rem(step + mats - 1, mats)

    return pl.pallas_call(
        functools.partial(output_kernel, experts, parts),
        grid=(mats,),
        in_specs=[pl.BlockSpec((1, stored, width), lambda i: (matrix(i), 0, 0))] * parts
        + [
            pl.BlockSpec((nx, top, many, share), lambda i: (0, matrix(i), 0, 0)),
            pl.BlockSpec((experts, top, total), lambda i: (0, 0, 0)),
        ],
        out_specs=pl.BlockSpec((ny, nh, 1, small, width), lambda i: (0, 0, (i + 1) // 2, 0, 0)),
        out_shape=pltpu.HBM((ny, nh, 2, small, width), BF16),
        scratch_shapes=[pltpu.VMEM((total, width), F32)],
        compiler_params=pltpu.CompilerParams(vmem_limit_bytes=VMEM_BYTES),
        cost_estimate=pl.CostEstimate(
            flops=2 * mats * parts * stored * width * total,
            bytes_accessed=2 * (mats * parts * stored * width + shared.size + 2 * total * width),
            transcendentals=0,
        ),
        name="output",
    )(*weights, shared, mask)


def gradient_kernel(experts, part, start, shared_ref, mask_ref, every_ref, out_ref, rows_ref, sems):
    rows = rows_ref.shape[1]
    load = pltpu.make_async_copy(every_ref.at[:, pl.ds(start, rows)], rows_ref, sems.at[0])

    @pl.when(pl.program_id(0) == 0)
    def _():
        load.start()
        load.wait()

    values = rows_ref[...].reshape(-1, rows_ref.shape[2])
    units = out_ref.shape[2] // experts
    for p in range(out_ref.shape[0]):
        wide = widen(shared_ref, mask_ref, experts, units, part + p)
        out_ref[p, 0] = jnp.dot(wide, values, preferred_element_type=F32).astype(BF16)


def gradient(shared, mask, everything, first, mats, part, parts, start, units, rows):
    experts, top, total = mask.shape
    nx, _, many, share = shared.shape
    ny, _, width = everything.shape
    stored = experts * units
    return pl.pallas_call(
        functools.partial(gradient_kernel, experts, part, start),
        grid=(mats,),
        in_specs=[
            pl.BlockSpec((nx, top, many, share), lambda m: (0, first + m, 0, 0)),
            pl.BlockSpec((experts, top, total), lambda m: (0, 0, 0)),
            whole(pltpu.HBM),
        ],
        out_specs=pl.BlockSpec((parts, 1, stored, width), lambda m: (0, m, 0, 0)),
        out_shape=jax.ShapeDtypeStruct((parts, mats, stored, width), BF16),
        scratch_shapes=[pltpu.VMEM((ny, rows, width), BF16), pltpu.SemaphoreType.DMA((1,))],
        compiler_params=pltpu.CompilerParams(vmem_limit_bytes=VMEM_BYTES),
        cost_estimate=pl.CostEstimate(
            flops=2 * mats * parts * stored * width * total,
            bytes_accessed=2 * (mats * parts * stored * width + shared.size + total * width),
            transcendentals=0,
        ),
        name="gradient",
    )(shared, mask, everything)


def body(tokens, slot_ids, gate_values, slot_expert, w_gate, w_up, w_down, cotangent):
    block, width = tokens.shape
    experts, units, _ = w_gate.shape
    ny, nh, nl, nx = (lax.axis_size(a) for a in ("y", "zh", "zl", "x"))
    top = slot_ids.shape[1]
    rows = block // nl
    total = ny * rows
    share = total // nx
    many = 2 * nl * units
    stored = experts * units

    def own_rows(value):
        return lax.dynamic_slice_in_dim(value, lax.axis_index("zl") * rows, rows, axis=0)

    ids, values = own_rows(slot_ids), own_rows(gate_values)
    numbers = jnp.arange(slot_expert.shape[0], dtype=jnp.int32)
    chosen = jnp.sum(
        jnp.where(ids[:, :, None] == numbers, slot_expert[None, None, :], 0), axis=-1
    ).astype(F32)
    part0 = short(values)
    part1 = short(values - part0)
    part2 = short(values - part0 - part1)
    meta = jnp.stack([chosen, part0, part1, part2]).transpose(0, 2, 1).astype(BF16)
    facts_of = 4 * top * rows
    meta = jnp.pad(meta.reshape(1, facts_of), ((0, 15), (0, width - facts_of)))
    packed = jnp.concatenate([own_rows(tokens), own_rows(cotangent), meta], axis=0)
    held = packed.shape[0]
    everything = lax.all_gather(packed, "y", axis=0, tiled=True).reshape(ny, held, width)

    own = jnp.stack([w_gate, w_up, w_down]).reshape(3, stored, width)
    near = swap(own, "zl")
    weights = [own, near, swap(own, "core"), swap(near, "core")]

    facts = everything[:, 2 * rows, :facts_of].reshape(ny, 4, top, rows).astype(F32)
    facts = facts.transpose(1, 2, 0, 3).reshape(4, top, total)
    scale = facts[1] + facts[2] + facts[3]
    mask = (facts[0][None] == jnp.arange(experts, dtype=F32)[:, None, None]).astype(F32)
    own_scale = lax.dynamic_slice_in_dim(scale, lax.axis_index("x") * share, share, axis=1)

    def exchange(value):
        return lax.all_to_all(value, "x", split_axis=0, concat_axis=0, tiled=True)

    mask, own_scale = lax.optimization_barrier((mask, own_scale))
    picked = pick(weights, experts, everything, mask, rows, nx)
    shared = exchange(middle(exchange(picked), own_scale))
    parts = output(shared, weights, experts, mask, ny, nh)
    small = rows // nh
    parts, shared = lax.optimization_barrier((parts, shared))
    scattered = lax.psum_scatter(
        parts.reshape(ny * 2 * rows, width), "y", scatter_dimension=0, tiled=True
    )

    def product(first, mats, part):
        start = rows if first == 2 else 0
        return gradient(shared, mask, everything, first, mats, part, nl, start, units, rows)

    def near_of(kept, sent):
        return swap((kept[1].astype(F32) + sent[1].astype(F32)).astype(BF16), "zl")

    sent_down = product(2, 1, nl)
    sent_down, shared = lax.optimization_barrier((sent_down, shared))
    sent_down = swap(sent_down, "core")
    sent = product(0, 2, nl)
    sent, shared = lax.optimization_barrier((sent, shared))
    sent = swap(sent, "core")
    kept_down = product(2, 1, 0)
    near_down = near_of(kept_down, sent_down)
    kept = product(0, 2, 0)
    near = near_of(kept, sent)

    parts = scattered.reshape(nh, 2, small, width)
    parts = lax.all_to_all(parts, "zh", split_axis=0, concat_axis=0, tiled=True)
    parts = jnp.sum(parts.astype(F32), axis=0).astype(BF16)
    copies = jnp.broadcast_to(parts[None], (nh * nl,) + parts.shape)
    copies, near_down, near = lax.optimization_barrier((copies, near_down, near))
    ends = lax.all_to_all(copies, ("zh", "zl"), split_axis=0, concat_axis=0, tiled=True)
    ends = ends.reshape(nh, nl, 2, small, width).transpose(2, 1, 0, 3, 4).reshape(2, block, width)

    def finish(kept, sent, near):
        done = sum(value.astype(F32) for value in (kept[0], sent[0], near)).astype(BF16)
        return done.reshape(-1, experts, units, width)

    (grad_down,) = finish(kept_down, sent_down, near_down)
    grad_gate, grad_up = finish(kept, sent, near)

    return (ends[0], ends[1], grad_gate, grad_up, grad_down)


def solution(mesh):
    dp, ep, mp = mesh.shape["dp"], mesh.shape["expert"], mesh.shape["mp"]
    split = Mesh(
        mesh.devices.reshape(dp // 2, 2, ep // 2, 2, mp), ("y", "core", "zh", "zl", "x")
    )
    rows = ("y", "core")
    stored = P(None, ("y", "core", "zh", "zl"), "x")
    return jax.shard_map(
        body,
        mesh=split,
        in_specs=(
            P(rows, "x"),
            P(rows, None),
            P(rows, None),
            P(),
            stored,
            stored,
            stored,
            P(rows, "x"),
        ),
        out_specs=(P(rows, "x"), P(rows, "x"), stored, stored, stored),
        check_vma=False,
    )
```
